32 devices in a mesh: outer: 8 (over z, x), inner: 4 (over y, core).
Axes of the slice: x: 2, y: 2, z: 4, core: 2. Of those that a mesh axis runs over, the one named last changes fastest.
Arguments:
- features: bfloat16 [4096, 4096], P(('outer', 'inner')), may hold values from -6 to 6
- cotangent: bfloat16 [4096, 512], P(('outer', 'inner')), may hold values from -6 to 6
- w_codes: bfloat16 [1024, 4, 512], P('inner'), may hold values from -0.09375 to 0.09375
- w_scales: float32 [1024, 1, 1], P('inner'), may hold values from 0.4 to 2.5
Outputs:
- key_proj: bfloat16 [4096, 512], P(('outer', 'inner'))
- grad_input: bfloat16 [4096, 4096], P(('outer', 'inner'))
- grad_weight: bfloat16 [4096, 512], P(('inner', 'outer'))
The draws below stay inside these ranges and needn't reach their ends.
All inputs are finite; a program needn't handle non-finite values. Where the reference program divides by a largest or mean magnitude, that divisor is 1e-20 or more.
Results may differ from the reference program's by a relative error of at most 0.014.
Values may be sent and summed in bfloat16 or wider, within the bound.
A program may use at most 64 MiB of HBM per device.

```python
import math
import jax
import jax.numpy as jnp
from jax import lax

D_WIN = 4096
KV = 512
TOK_DEV = 128
ROWS_BLOCK = 4
BLOCKS_W = 1024
TOKENS = 4096
N_OUTER = 8
N_INNER = 4


def raised(drawn, rng, source, target, blocks, factor):
    owner, partner = [(jnp.arange(drawn.shape[axis_at]) // (drawn.shape[axis_at] // blocks)).reshape([-1 if axis == axis_at else 1 for axis in range(drawn.ndim)]) for axis_at in (source, target)]
    chosen = jax.random.permutation(rng, blocks)[partner]
    strong = (owner == chosen) | (owner == (partner + blocks // 2) % blocks)
    return jnp.where(strong, factor * drawn, drawn)


def shard_levels(rng, extent, split, least, high):
    level = 1.0
    for position, parts in split:
        draws = jax.random.uniform(jax.random.fold_in(jax.random.fold_in(rng, 6), position), (parts,), jnp.float32, least / len(split), high / len(split))
        level = level * jnp.repeat(jnp.exp(draws), extent[position] // parts).reshape((-1,) + (1,) * (len(extent) - 1 - position))
    return level


def scatter_about(own_key, extent, width, limit, shards=(), kind=jnp.bfloat16):
    drawn = width * jax.random.normal(own_key, extent, jnp.float32)
    if shards:
        drawn = drawn * shard_levels(own_key, extent, shards, -0.22, 0.18)
    return jnp.clip(drawn, -limit, limit).astype(kind)


def gaussian_with(own_key, shape, spread, bound, split, heavy, held_as=jnp.bfloat16):
    array = spread * jax.random.normal(own_key, shape, jnp.float32)
    if split:
        array = array * shard_levels(own_key, shape, split, -0.22, 0.18)
    return jnp.clip(raised(array, jax.random.fold_in(own_key, 3), *heavy), -bound, bound).astype(held_as)


def setup_inputs(seed: int = 0) -> dict:
    key_of = jax.random.split(jax.random.key(seed), 5)
    features = gaussian_with(key_of[0], (TOKENS, D_WIN), 1.0, 6.0, ((0, 32),), (0, 1, 32, 2.75))
    cotangent = scatter_about(key_of[1], (TOKENS, KV), 1.0, 6.0, ((0, 32),))
    w_codes = scatter_about(key_of[2], (BLOCKS_W, ROWS_BLOCK, KV), D_WIN ** -0.5, 0.09375, ((0, 4),))
    w_scales = jnp.clip(jnp.exp(math.log(2.5) - 1.8325814 * jax.random.uniform(key_of[3], (BLOCKS_W, 1, 1), jnp.float32) ** shard_levels(key_of[3], (BLOCKS_W, 1, 1), ((0, 4),), -0.2, 0.2)), 0.4, 2.5)
    return dict(features=features, cotangent=cotangent, w_codes=w_codes, w_scales=w_scales)


def reference(features, cotangent, w_codes, w_scales):
    weight = (w_codes.astype(jnp.float32) * w_scales).astype(jnp.bfloat16).reshape(D_WIN, KV)
    key_proj = jnp.dot(features, weight, preferred_element_type=jnp.float32).astype(jnp.bfloat16)
    grad_input = jnp.dot(cotangent, weight.T, preferred_element_type=jnp.float32).astype(jnp.bfloat16)
    feat_groups = features.reshape(N_OUTER, N_INNER, TOK_DEV, D_WIN)
    cot_groups = cotangent.reshape(N_OUTER, N_INNER, TOK_DEV, KV)

    def outer_step(running, slices):
        feat_outer, cot_outer = slices

        def inner_step(summed, member):
            feat_member, cot_member = member
            partial_value = lax.dot_general(feat_member, cot_member, (((0,), (0,)), ((), ())), preferred_element_type=jnp.float32)
            rounded = lax.optimization_barrier(partial_value.astype(jnp.bfloat16))
            return summed + rounded.astype(jnp.float32), None

        group_sum, unused = lax.scan(inner_step, jnp.zeros((D_WIN, KV), jnp.float32), (feat_outer, cot_outer))
        blocks = group_sum.reshape(BLOCKS_W, ROWS_BLOCK * KV)
        block_scale = jnp.max(jnp.abs(blocks), axis=1, keepdims=True) + 1e-6
        block_codes = lax.optimization_barrier((blocks / block_scale).astype(jnp.bfloat16))
        return running + block_codes.astype(jnp.float32) * block_scale, None

    running, unused = lax.scan(outer_step, jnp.zeros((BLOCKS_W, ROWS_BLOCK * KV), jnp.float32), (feat_groups, cot_groups))
    grad_weight = (running / (N_OUTER * N_INNER)).reshape(D_WIN, KV).astype(jnp.bfloat16)
    return key_proj, grad_input, grad_weight
```

```python
import functools

import jax
import jax.numpy as jnp
from jax import lax
from jax.experimental import pallas as pl
from jax.experimental.pallas import tpu as pltpu
from jax.sharding import PartitionSpec as P


def dequantize(codes, scales):
    width = codes.shape[2]
    return (codes.astype(jnp.float32) * scales).astype(jnp.bfloat16).reshape(-1, width)


def forward_part(features, cotangent, w_codes, w_scales):
    weight = lax.all_gather(dequantize(w_codes, w_scales), "inner", axis=0, tiled=True)
    key_proj = jnp.dot(features, weight, preferred_element_type=jnp.float32).astype(jnp.bfloat16)
    grad_input = lax.dot_general(
        cotangent, weight, (((1,), (1,)), ((), ())), preferred_element_type=jnp.float32
    ).astype(jnp.bfloat16)
    return (key_proj, grad_input)


def gradient_part(features, cotangent, rows_block):
    width = cotangent.shape[1]
    grad_share = lax.psum_scatter(
        lax.dot_general(
            features, cotangent, (((0,), (0,)), ((), ())), preferred_element_type=jnp.float32
        ).astype(jnp.bfloat16),
        "inner",
        scatter_dimension=0,
        tiled=True,
    ).astype(jnp.float32)
    blocks = grad_share.reshape(-1, rows_block * width)
    block_scale = jnp.max(jnp.abs(blocks), axis=1, keepdims=True) + 1e-06
    block_codes = (blocks / block_scale).astype(jnp.bfloat16).reshape(-1, rows_block, width)
    got_codes, got_scales = (
        lax.all_to_all(block_codes, "outer", split_axis=0, concat_axis=0, tiled=True),
        lax.all_to_all(
            block_scale.reshape(-1, 1, 1).astype(jnp.bfloat16),
            "outer",
            split_axis=0,
            concat_axis=0,
            tiled=True,
        ).astype(jnp.float32),
    )
    senders = lax.axis_size("outer")
    devices = senders * lax.axis_size("inner")
    restored = (got_codes.astype(jnp.float32) * got_scales).reshape(senders, -1, rows_block, width)
    summed = jnp.sum(restored, axis=0).reshape(-1, width)
    return (summed / devices).astype(jnp.bfloat16)


def on_device(features, cotangent, w_codes, w_scales):
    rows_block = w_codes.shape[1]
    key_proj, grad_input = forward_part(features, cotangent, w_codes, w_scales)
    grad_weight = gradient_part(features, cotangent, rows_block)
    return (key_proj, grad_input, grad_weight)


WEIGHT_OF = {"y": 16, "core": 8, "zh": 4, "zl": 2, "x": 1}
STREAMS = (("core", "x", "y", "zl", "zh"), ("core", "zl", "y", "x", "zh"))
MESH = pl.DeviceIdType.MESH


def kernel(feat, cot, own, key_ref, gin_ref, gw_ref, part, got, held, acc, w_send, w_recv, g_send, g_recv):
    outer, inner = lax.axis_index("outer"), lax.axis_index("inner")
    bit = {
        "x": outer % 2,
        "zl": (outer // 2) % 2,
        "zh": outer // 4,
        "core": inner % 2,
        "y": inner // 2,
    }

    def flip(v, b, step):
        return v + step - 2 * step * b

    partner = {
        "x": (flip(outer, bit["x"], 1), inner),
        "zl": (flip(outer, bit["zl"], 2), inner),
        "zh": (flip(outer, bit["zh"], 4), inner),
        "core": (outer, flip(inner, bit["core"], 1)),
        "y": (outer, flip(inner, bit["y"], 2)),
    }
    barrier = pltpu.get_barrier_semaphore()
    for p in partner.values():
        pl.semaphore_signal(barrier, inc=1, device_id=p, device_id_type=MESH)
    pl.semaphore_wait(barrier, len(partner))

    rows = part.shape[2]
    cols = part.shape[3]
    half = own.shape[1]
    mine = bit["x"]
    other = 1 - mine

    def remote(src, dst, send, recv, dim):
        return pltpu.make_async_remote_copy(
            src_ref=src, dst_ref=dst, send_sem=send, recv_sem=recv,
            device_id=partner[dim], device_id_type=MESH,
        )

    def w_copy(n, src, dst, dim):
        return remote(src, dst, w_send.at[n], w_recv.at[n], dim)

    def g_copy(s, step):
        n = 16 >> step
        return remote(
            part.at[s, pl.ds(n, n)], got.at[s, pl.ds(n, n)],
            g_send.at[s, step], g_recv.at[s, step], STREAMS[s][step],
        )

    over_y = w_copy(0, own.at[mine], held.at[1, mine], "y")
    over_core = w_copy(1, own, held.at[0], "core")
    over_x = w_copy(2, held.at[1, mine], held.at[1, mine], "x")
    core_mine = w_copy(3, held.at[1, mine], held.at[2, mine], "core")
    core_other = w_copy(4, held.at[1, other], held.at[2, other], "core")
    g = [[g_copy(s, step) for step in range(5)] for s in range(2)]

    over_y.start()

    def partial(n):
        rel, rest = {}, n
        for dim in reversed(STREAMS[0]):
            rel[dim] = rest % 2
            rest = rest // 2
        block = 0
        for dim, w in WEIGHT_OF.items():
            block = block + w * (rel[dim] + bit[dim] - 2 * rel[dim] * bit[dim])
        second = 0
        for dim in STREAMS[1]:
            second = second * 2 + rel[dim]
        at = pl.multiple_of(block * rows, rows)
        value = lax.dot_general(
            feat[:, pl.ds(at, rows)], cot[...], (((0,), (0,)), ((), ())),
            preferred_element_type=jnp.float32,
        ).astype(jnp.bfloat16)
        part[0, n] = value[:, :cols]
        part[1, second] = value[:, cols:]

    for n in range(16, 32):
        partial(n)
    g[0][0].start()
    g[1][0].start()
    over_core.start()
    for n in range(16):
        partial(n)

    def add(s, lo, n, base):
        @pl.loop(lo, lo + n)
        def _(j):
            part[s, j] = (
                part[s, j].astype(jnp.float32) + got[s, base + j].astype(jnp.float32)
            ).astype(jnp.bfloat16)

    def advance(s, step):
        n = 16 >> step
        g[s][step].wait_recv()
        add(s, n // 2, n // 2, n)
        g[s][step + 1].start()
        add(s, 0, n // 2, n)

    def finish(s):
        g[s][4].wait_recv()
        total = part[s, 0].astype(jnp.float32) + got[s, 1].astype(jnp.float32)
        devices = lax.axis_size("outer") * lax.axis_size("inner")
        gw_ref[:, s * cols:(s + 1) * cols] = (total / devices).astype(jnp.bfloat16)

    flipped_core = flip(inner, bit["core"], 1)
    flipped_y = flip(inner, bit["y"], 2)
    flipped_both = flip(flipped_core, bit["y"], 2)

    def unit(block, shard, h, first=False):
        at = pl.multiple_of((shard * 2 + h) * half, half)
        value = jnp.dot(feat[:, pl.ds(at, half)], block[...], preferred_element_type=jnp.float32)
        acc[...] = value if first else acc[...] + value
        gin_ref[:, pl.ds(at, half)] = lax.dot_general(
            cot[...], block[...], (((1,), (1,)), ((), ())), preferred_element_type=jnp.float32
        ).astype(jnp.bfloat16)

    advance(0, 0)
    advance(1, 0)
    unit(own.at[0], inner, 0, first=True)
    unit(own.at[1], inner, 1)
    over_core.wait_recv()
    unit(held.at[0, 0], flipped_core, 0)
    unit(held.at[0, 1], flipped_core, 1)
    over_y.wait_recv()
    over_x.start()
    core_mine.start()
    unit(held.at[1, mine], flipped_y, mine)
    advance(0, 1)
    advance(1, 1)
    core_mine.wait_recv()
    unit(held.at[2, mine], flipped_both, mine)
    advance(0, 2)
    advance(1, 2)
    over_x.wait_recv()
    core_other.start()
    advance(0, 3)
    advance(1, 3)
    unit(held.at[1, other], flipped_y, other)
    core_other.wait_recv()
    unit(held.at[2, other], flipped_both, other)
    key_ref[...] = acc[...].astype(jnp.bfloat16)
    finish(0)
    finish(1)
    for copy in (over_y, over_core, over_x, core_mine, core_other, *g[0], *g[1]):
        copy.wait_send()


def fused(features, cotangent, w_codes, w_scales):
    tokens, depth = features.shape
    width = cotangent.shape[1]
    weight = dequantize(w_codes, w_scales)
    half = weight.shape[0] // 2
    rows = depth // 32
    cols = width // 2
    bf16 = jnp.bfloat16
    vmem = pl.BlockSpec(memory_space=pltpu.VMEM)
    return pl.pallas_call(
        kernel,
        out_shape=(
            jax.ShapeDtypeStruct((tokens, width), bf16),
            jax.ShapeDtypeStruct((tokens, depth), bf16),
            jax.ShapeDtypeStruct((rows, width), bf16),
        ),
        in_specs=[vmem] * 3,
        out_specs=(vmem,) * 3,
        scratch_shapes=[
            pltpu.VMEM((2, 32, rows, cols), bf16),
            pltpu.VMEM((2, 32, rows, cols), bf16),
            pltpu.VMEM((3, 2, half, width), bf16),
            pltpu.VMEM((tokens, width), jnp.float32),
            pltpu.SemaphoreType.DMA((5,)),
            pltpu.SemaphoreType.DMA((5,)),
            pltpu.SemaphoreType.DMA((2, 5)),
            pltpu.SemaphoreType.DMA((2, 5)),
        ],
        compiler_params=pltpu.CompilerParams(
            collective_id=0, has_side_effects=True, vmem_limit_bytes=40 * 1024 * 1024
        ),
        cost_estimate=pl.CostEstimate(
            flops=6 * tokens * depth * width, bytes_accessed=8 * tokens * depth, transcendentals=0
        ),
    )(features, cotangent, weight.reshape(2, half, width))


def solution(mesh):
    in_specs = (
        P(("outer", "inner"), None),
        P(("outer", "inner"), None),
        P("inner", None, None),
        P("inner", None, None),
    )
    out_specs = (
        P(("outer", "inner"), None),
        P(("outer", "inner"), None),
        P(("inner", "outer"), None),
    )
    small = mesh.shape["outer"] == 8 and mesh.shape["inner"] == 4
    return jax.shard_map(
        fused if small else on_device,
        mesh=mesh, in_specs=in_specs, out_specs=out_specs, check_vma=False,
    )
```

```python
import functools

import jax
import jax.numpy as jnp
from jax import lax
from jax.experimental import pallas as pl
from jax.experimental.pallas import tpu as pltpu
from jax.sharding import PartitionSpec as P


def dequantize(codes, scales):
    width = codes.shape[2]
    return (codes.astype(jnp.float32) * scales).astype(jnp.bfloat16).reshape(-1, width)


def forward_part(features, cotangent, w_codes, w_scales):
    weight = lax.all_gather(dequantize(w_codes, w_scales), "inner", axis=0, tiled=True)
    key_proj = jnp.dot(features, weight, preferred_element_type=jnp.float32).astype(jnp.bfloat16)
    grad_input = lax.dot_general(
        cotangent, weight, (((1,), (1,)), ((), ())), preferred_element_type=jnp.float32
    ).astype(jnp.bfloat16)
    return (key_proj, grad_input)


def gradient_part(features, cotangent, rows_block):
    width = cotangent.shape[1]
    grad_share = lax.psum_scatter(
        lax.dot_general(
            features, cotangent, (((0,), (0,)), ((), ())), preferred_element_type=jnp.float32
        ).astype(jnp.bfloat16),
        "inner",
        scatter_dimension=0,
        tiled=True,
    ).astype(jnp.float32)
    blocks = grad_share.reshape(-1, rows_block * width)
    block_scale = jnp.max(jnp.abs(blocks), axis=1, keepdims=True) + 1e-06
    block_codes = (blocks / block_scale).astype(jnp.bfloat16).reshape(-1, rows_block, width)
    got_codes, got_scales = (
        lax.all_to_all(block_codes, "outer", split_axis=0, concat_axis=0, tiled=True),
        lax.all_to_all(
            block_scale.reshape(-1, 1, 1).astype(jnp.bfloat16),
            "outer",
            split_axis=0,
            concat_axis=0,
            tiled=True,
        ).astype(jnp.float32),
    )
    senders = lax.axis_size("outer")
    devices = senders * lax.axis_size("inner")
    restored = (got_codes.astype(jnp.float32) * got_scales).reshape(senders, -1, rows_block, width)
    summed = jnp.sum(restored, axis=0).reshape(-1, width)
    return (summed / devices).astype(jnp.bfloat16)


def on_device(features, cotangent, w_codes, w_scales):
    rows_block = w_codes.shape[1]
    key_proj, grad_input = forward_part(features, cotangent, w_codes, w_scales)
    grad_weight = gradient_part(features, cotangent, rows_block)
    return (key_proj, grad_input, grad_weight)


WEIGHT_OF = {"y": 16, "core": 8, "zh": 4, "zl": 2, "x": 1}
STREAMS = (
    ("core", "x", "y", "zl", "zh"),
    ("core", "zl", "y", "x", "zh"),
    ("core", "x", "zl", "y", "zh"),
    ("core", "zl", "x", "y", "zh"),
)
MESH = pl.DeviceIdType.MESH


def kernel(feat, cot, own, key_ref, gin_ref, gw_ref, part, got, held, acc, w_send, w_recv, g_send, g_recv):
    outer, inner = lax.axis_index("outer"), lax.axis_index("inner")
    bit = {
        "x": outer % 2,
        "zl": (outer // 2) % 2,
        "zh": outer // 4,
        "core": inner % 2,
        "y": inner // 2,
    }

    def flip(v, b, step):
        return v + step - 2 * step * b

    partner = {
        "x": (flip(outer, bit["x"], 1), inner),
        "zl": (flip(outer, bit["zl"], 2), inner),
        "zh": (flip(outer, bit["zh"], 4), inner),
        "core": (outer, flip(inner, bit["core"], 1)),
        "y": (outer, flip(inner, bit["y"], 2)),
    }
    barrier = pltpu.get_barrier_semaphore()
    for p in partner.values():
        pl.semaphore_signal(barrier, inc=1, device_id=p, device_id_type=MESH)
    pl.semaphore_wait(barrier, len(partner))

    rows = part.shape[2]
    cols = part.shape[3]
    half = own.shape[1]
    mine = bit["x"]
    other = 1 - mine

    def remote(src, dst, send, recv, dim):
        return pltpu.make_async_remote_copy(
            src_ref=src, dst_ref=dst, send_sem=send, recv_sem=recv,
            device_id=partner[dim], device_id_type=MESH,
        )

    def w_copy(n, src, dst, dim):
        return remote(src, dst, w_send.at[n], w_recv.at[n], dim)

    def g_copy(s, sem, step, at, n):
        return remote(
            part.at[s, pl.ds(at, n)], got.at[s, pl.ds(at, n)],
            g_send.at[s, sem], g_recv.at[s, sem], STREAMS[s][step],
        )

    over_y = w_copy(0, own.at[mine], held.at[1, mine], "y")
    over_core = w_copy(1, own, held.at[0], "core")
    over_x = w_copy(2, held.at[1, mine], held.at[1, mine], "x")
    core_mine = w_copy(3, held.at[1, mine], held.at[2, mine], "core")
    core_other = w_copy(4, held.at[1, other], held.at[2, other], "core")
    streams = range(len(STREAMS))
    first = [g_copy(s, 5, 0, 24, 8) for s in streams]
    g = [
        [g_copy(s, step, step, 16 >> step, 8 if step == 0 else 16 >> step) for step in range(5)]
        for s in streams
    ]

    over_y.start()

    def partial(n):
        rel, rest = {}, n
        for dim in reversed(STREAMS[0]):
            rel[dim] = rest % 2
            rest = rest // 2
        block = 0
        for dim, w in WEIGHT_OF.items():
            block = block + w * (rel[dim] + bit[dim] - 2 * rel[dim] * bit[dim])
        at = pl.multiple_of(block * rows, rows)
        value = lax.dot_general(
            feat[:, pl.ds(at, rows)], cot[...], (((0,), (0,)), ((), ())),
            preferred_element_type=jnp.float32,
        ).astype(jnp.bfloat16)
        for s, order in enumerate(STREAMS):
            place = 0
            for dim in order:
                place = place * 2 + rel[dim]
            part[s, place] = value[:, s * cols:(s + 1) * cols]

    for n in range(24, 32):
        partial(n)
    first[0].start()
    first[2].start()
    for n in (18, 19, 22, 23):
        partial(n)
    first[1].start()
    first[3].start()
    for n in (16, 17, 20, 21):
        partial(n)
    for s in streams:
        g[s][0].start()
    over_core.start()
    for n in range(16):
        partial(n)

    def add(s, lo, n, base):
        @pl.loop(lo, lo + n)
        def _(j):
            part[s, j] = (
                part[s, j].astype(jnp.float32) + got[s, base + j].astype(jnp.float32)
            ).astype(jnp.bfloat16)

    def advance(s, step):
        n = 16 >> step
        (first[s] if step == 0 else g[s][step]).wait_recv()
        add(s, n // 2, n // 2, n)
        g[s][step + 1].start()
        if step == 0:
            g[s][0].wait_recv()
        add(s, 0, n // 2, n)

    def finish(s):
        g[s][4].wait_recv()
        total = part[s, 0].astype(jnp.float32) + got[s, 1].astype(jnp.float32)
        devices = lax.axis_size("outer") * lax.axis_size("inner")
        gw_ref[:, s * cols:(s + 1) * cols] = (total / devices).astype(jnp.bfloat16)

    flipped_core = flip(inner, bit["core"], 1)
    flipped_y = flip(inner, bit["y"], 2)
    flipped_both = flip(flipped_core, bit["y"], 2)

    def unit(block, shard, h, first=False):
        at = pl.multiple_of((shard * 2 + h) * half, half)
        value = jnp.dot(feat[:, pl.ds(at, half)], block[...], preferred_element_type=jnp.float32)
        acc[...] = value if first else acc[...] + value
        gin_ref[:, pl.ds(at, half)] = lax.dot_general(
            cot[...], block[...], (((1,), (1,)), ((), ())), preferred_element_type=jnp.float32
        ).astype(jnp.bfloat16)

    def advance_all(step):
        for s in streams:
            advance(s, step)

    advance_all(0)
    unit(own.at[0], inner, 0, first=True)
    unit(own.at[1], inner, 1)
    over_core.wait_recv()
    unit(held.at[0, 0], flipped_core, 0)
    unit(held.at[0, 1], flipped_core, 1)
    over_y.wait_recv()
    over_x.start()
    core_mine.start()
    unit(held.at[1, mine], flipped_y, mine)
    advance_all(1)
    core_mine.wait_recv()
    unit(held.at[2, mine], flipped_both, mine)
    advance_all(2)
    over_x.wait_recv()
    core_other.start()
    advance_all(3)
    unit(held.at[1, other], flipped_y, other)
    core_other.wait_recv()
    unit(held.at[2, other], flipped_both, other)
    key_ref[...] = acc[...].astype(jnp.bfloat16)
    for s in streams:
        finish(s)
    for copy in (over_y, over_core, over_x, core_mine, core_other, *first, *sum(g, [])):
        copy.wait_send()


def fused(features, cotangent, w_codes, w_scales):
    tokens, depth = features.shape
    width = cotangent.shape[1]
    weight = dequantize(w_codes, w_scales)
    half = weight.shape[0] // 2
    rows = depth // 32
    cols = width // len(STREAMS)
    bf16 = jnp.bfloat16
    vmem = pl.BlockSpec(memory_space=pltpu.VMEM)
    return pl.pallas_call(
        kernel,
        out_shape=(
            jax.ShapeDtypeStruct((tokens, width), bf16),
            jax.ShapeDtypeStruct((tokens, depth), bf16),
            jax.ShapeDtypeStruct((rows, width), bf16),
        ),
        in_specs=[vmem] * 3,
        out_specs=(vmem,) * 3,
        scratch_shapes=[
            pltpu.VMEM((len(STREAMS), 32, rows, cols), bf16),
            pltpu.VMEM((len(STREAMS), 32, rows, cols), bf16),
            pltpu.VMEM((3, 2, half, width), bf16),
            pltpu.VMEM((tokens, width), jnp.float32),
            pltpu.SemaphoreType.DMA((5,)),
            pltpu.SemaphoreType.DMA((5,)),
            pltpu.SemaphoreType.DMA((len(STREAMS), 6)),
            pltpu.SemaphoreType.DMA((len(STREAMS), 6)),
        ],
        compiler_params=pltpu.CompilerParams(
            collective_id=0, has_side_effects=True, vmem_limit_bytes=40 * 1024 * 1024
        ),
        cost_estimate=pl.CostEstimate(
            flops=6 * tokens * depth * width, bytes_accessed=8 * tokens * depth, transcendentals=0
        ),
    )(features, cotangent, weight.reshape(2, half, width))


def solution(mesh):
    in_specs = (
        P(("outer", "inner"), None),
        P(("outer", "inner"), None),
        P("inner", None, None),
        P("inner", None, None),
    )
    out_specs = (
        P(("outer", "inner"), None),
        P(("outer", "inner"), None),
        P(("inner", "outer"), None),
    )
    small = mesh.shape["outer"] == 8 and mesh.shape["inner"] == 4
    return jax.shard_map(
        fused if small else on_device,
        mesh=mesh, in_specs=in_specs, out_specs=out_specs, check_vma=False,
    )
```

```python
import functools

import jax
import jax.numpy as jnp
from jax import lax
from jax.experimental import pallas as pl
from jax.experimental.pallas import tpu as pltpu
from jax.sharding import PartitionSpec as P


def dequantize(codes, scales):
    width = codes.shape[2]
    return (codes.astype(jnp.float32) * scales).astype(jnp.bfloat16).reshape(-1, width)


def forward_part(features, cotangent, w_codes, w_scales):
    weight = lax.all_gather(dequantize(w_codes, w_scales), "inner", axis=0, tiled=True)
    key_proj = jnp.dot(features, weight, preferred_element_type=jnp.float32).astype(jnp.bfloat16)
    grad_input = lax.dot_general(
        cotangent, weight, (((1,), (1,)), ((), ())), preferred_element_type=jnp.float32
    ).astype(jnp.bfloat16)
    return (key_proj, grad_input)


def gradient_part(features, cotangent, rows_block):
    width = cotangent.shape[1]
    grad_share = lax.psum_scatter(
        lax.dot_general(
            features, cotangent, (((0,), (0,)), ((), ())), preferred_element_type=jnp.float32
        ).astype(jnp.bfloat16),
        "inner",
        scatter_dimension=0,
        tiled=True,
    ).astype(jnp.float32)
    blocks = grad_share.reshape(-1, rows_block * width)
    block_scale = jnp.max(jnp.abs(blocks), axis=1, keepdims=True) + 1e-06
    block_codes = (blocks / block_scale).astype(jnp.bfloat16).reshape(-1, rows_block, width)
    got_codes, got_scales = (
        lax.all_to_all(block_codes, "outer", split_axis=0, concat_axis=0, tiled=True),
        lax.all_to_all(
            block_scale.reshape(-1, 1, 1).astype(jnp.bfloat16),
            "outer",
            split_axis=0,
            concat_axis=0,
            tiled=True,
        ).astype(jnp.float32),
    )
    senders = lax.axis_size("outer")
    devices = senders * lax.axis_size("inner")
    restored = (got_codes.astype(jnp.float32) * got_scales).reshape(senders, -1, rows_block, width)
    summed = jnp.sum(restored, axis=0).reshape(-1, width)
    return (summed / devices).astype(jnp.bfloat16)


def on_device(features, cotangent, w_codes, w_scales):
    rows_block = w_codes.shape[1]
    key_proj, grad_input = forward_part(features, cotangent, w_codes, w_scales)
    grad_weight = gradient_part(features, cotangent, rows_block)
    return (key_proj, grad_input, grad_weight)


WEIGHT_OF = {"y": 16, "core": 8, "zh": 4, "zl": 2, "x": 1}
STREAMS = (
    ("core", "x", "y", "zl", "zh"),
    ("core", "zl", "y", "x", "zh"),
    ("core", "x", "zl", "y", "zh"),
    ("core", "zl", "x", "y", "zh"),
)
CHUNKS = 4
MESH = pl.DeviceIdType.MESH


def kernel(feat, cot, own, key_ref, gin_ref, gw_ref, part, got, held, acc, w_send, w_recv, g_send, g_recv):
    outer, inner = lax.axis_index("outer"), lax.axis_index("inner")
    bit = {
        "x": outer % 2,
        "zl": (outer // 2) % 2,
        "zh": outer // 4,
        "core": inner % 2,
        "y": inner // 2,
    }

    def flip(v, b, step):
        return v + step - 2 * step * b

    partner = {
        "x": (flip(outer, bit["x"], 1), inner),
        "zl": (flip(outer, bit["zl"], 2), inner),
        "zh": (flip(outer, bit["zh"], 4), inner),
        "core": (outer, flip(inner, bit["core"], 1)),
        "y": (outer, flip(inner, bit["y"], 2)),
    }
    barrier = pltpu.get_barrier_semaphore()
    for p in partner.values():
        pl.semaphore_signal(barrier, inc=1, device_id=p, device_id_type=MESH)
    pl.semaphore_wait(barrier, len(partner))

    rows = part.shape[2]
    cols = part.shape[3]
    half = own.shape[1]
    mine = bit["x"] + bit["zl"] - 2 * bit["x"] * bit["zl"]
    other = 1 - mine

    def remote(src, dst, send, recv, dim):
        return pltpu.make_async_remote_copy(
            src_ref=src, dst_ref=dst, send_sem=send, recv_sem=recv,
            device_id=partner[dim], device_id_type=MESH,
        )

    def w_copy(n, src, dst, dim):
        return remote(src, dst, w_send.at[n], w_recv.at[n], dim)

    def g_copy(s, sem, step, at, n):
        return remote(
            part.at[s, pl.ds(at, n)], got.at[s, pl.ds(at, n)],
            g_send.at[s, sem], g_recv.at[s, sem], STREAMS[s][step],
        )

    def chunk(ref, h, c):
        return ref.at[h, pl.ds(c * (half // CHUNKS), half // CHUNKS)]

    chunks = range(CHUNKS)
    over_core = w_copy(4 * CHUNKS, own, held.at[0], "core")
    over_y = [w_copy(c, chunk(own, mine, c), chunk(held.at[1], mine, c), "y") for c in chunks]
    onward = [
        w_copy(
            CHUNKS + c, chunk(held.at[1], mine, c), chunk(held.at[1], mine, c), ("x", "zl")[c % 2]
        )
        for c in chunks
    ]
    core_mine, core_other = [
        [
            w_copy((2 + k) * CHUNKS + c, chunk(held.at[1], h, c), chunk(held.at[2], h, c), "core")
            for c in chunks
        ]
        for k, h in enumerate((mine, other))
    ]
    streams = range(len(STREAMS))
    first = [g_copy(s, 5, 0, 24, 8) for s in streams]
    g = [
        [g_copy(s, step, step, 16 >> step, 8 if step == 0 else 16 >> step) for step in range(5)]
        for s in streams
    ]

    for c in chunks:
        over_y[c].start()

    def forward(c):
        over_y[c].wait_recv()
        onward[c].start()
        core_mine[c].start()

    def across(c):
        onward[c].wait_recv()
        core_other[c].start()

    def partial(n):
        rel, rest = {}, n
        for dim in reversed(STREAMS[0]):
            rel[dim] = rest % 2
            rest = rest // 2
        block = 0
        for dim, w in WEIGHT_OF.items():
            block = block + w * (rel[dim] + bit[dim] - 2 * rel[dim] * bit[dim])
        at = pl.multiple_of(block * rows, rows)
        value = lax.dot_general(
            feat[:, pl.ds(at, rows)], cot[...], (((0,), (0,)), ((), ())),
            preferred_element_type=jnp.float32,
        ).astype(jnp.bfloat16)
        for s, order in enumerate(STREAMS):
            place = 0
            for dim in order:
                place = place * 2 + rel[dim]
            part[s, place] = value[:, s * cols:(s + 1) * cols]

    for n in range(24, 32):
        partial(n)
    first[0].start()
    first[2].start()
    for n in (18, 19, 22, 23):
        partial(n)
    first[1].start()
    first[3].start()
    for n in (16, 17, 20, 21):
        partial(n)
    for s in streams:
        g[s][0].start()
    over_core.start()
    for n in range(16):
        partial(n)

    def add(s, lo, n, base):
        @pl.loop(lo, lo + n)
        def _(j):
            part[s, j] = (
                part[s, j].astype(jnp.float32) + got[s, base + j].astype(jnp.float32)
            ).astype(jnp.bfloat16)

    def advance(s, step):
        n = 16 >> step
        (first[s] if step == 0 else g[s][step]).wait_recv()
        add(s, n // 2, n // 2, n)
        g[s][step + 1].start()
        if step == 0:
            g[s][0].wait_recv()
        add(s, 0, n // 2, n)

    def finish(s):
        g[s][4].wait_recv()
        total = part[s, 0].astype(jnp.float32) + got[s, 1].astype(jnp.float32)
        devices = lax.axis_size("outer") * lax.axis_size("inner")
        gw_ref[:, s * cols:(s + 1) * cols] = (total / devices).astype(jnp.bfloat16)

    flipped_core = flip(inner, bit["core"], 1)
    flipped_y = flip(inner, bit["y"], 2)
    flipped_both = flip(flipped_core, bit["y"], 2)

    def unit(block, shard, h, first=False):
        at = pl.multiple_of((shard * 2 + h) * half, half)
        value = jnp.dot(feat[:, pl.ds(at, half)], block[...], preferred_element_type=jnp.float32)
        acc[...] = value if first else acc[...] + value
        gin_ref[:, pl.ds(at, half)] = lax.dot_general(
            cot[...], block[...], (((1,), (1,)), ((), ())), preferred_element_type=jnp.float32
        ).astype(jnp.bfloat16)

    def advance_all(step):
        for s in streams:
            advance(s, step)

    forward(0)
    advance_all(0)
    forward(1)
    unit(own.at[0], inner, 0, first=True)
    unit(own.at[1], inner, 1)
    over_core.wait_recv()
    unit(held.at[0, 0], flipped_core, 0)
    unit(held.at[0, 1], flipped_core, 1)
    for c in range(2, CHUNKS):
        forward(c)
    unit(held.at[1, mine], flipped_y, mine)
    advance_all(1)
    for c in chunks:
        core_mine[c].wait_recv()
    unit(held.at[2, mine], flipped_both, mine)
    across(0)
    across(1)
    advance_all(2)
    for c in range(2, CHUNKS):
        across(c)
    advance_all(3)
    unit(held.at[1, other], flipped_y, other)
    for c in chunks:
        core_other[c].wait_recv()
    unit(held.at[2, other], flipped_both, other)
    key_ref[...] = acc[...].astype(jnp.bfloat16)
    for s in streams:
        finish(s)
    for copy in (over_core, *over_y, *onward, *core_mine, *core_other, *first, *sum(g, [])):
        copy.wait_send()


def fused(features, cotangent, w_codes, w_scales):
    tokens, depth = features.shape
    width = cotangent.shape[1]
    weight = dequantize(w_codes, w_scales)
    half = weight.shape[0] // 2
    rows = depth // 32
    cols = width // len(STREAMS)
    bf16 = jnp.bfloat16
    vmem = pl.BlockSpec(memory_space=pltpu.VMEM)
    return pl.pallas_call(
        kernel,
        out_shape=(
            jax.ShapeDtypeStruct((tokens, width), bf16),
            jax.ShapeDtypeStruct((tokens, depth), bf16),
            jax.ShapeDtypeStruct((rows, width), bf16),
        ),
        in_specs=[vmem] * 3,
        out_specs=(vmem,) * 3,
        scratch_shapes=[
            pltpu.VMEM((len(STREAMS), 32, rows, cols), bf16),
            pltpu.VMEM((len(STREAMS), 32, rows, cols), bf16),
            pltpu.VMEM((3, 2, half, width), bf16),
            pltpu.VMEM((tokens, width), jnp.float32),
            pltpu.SemaphoreType.DMA((4 * CHUNKS + 1,)),
            pltpu.SemaphoreType.DMA((4 * CHUNKS + 1,)),
            pltpu.SemaphoreType.DMA((len(STREAMS), 6)),
            pltpu.SemaphoreType.DMA((len(STREAMS), 6)),
        ],
        compiler_params=pltpu.CompilerParams(
            collective_id=0, has_side_effects=True, vmem_limit_bytes=40 * 1024 * 1024
        ),
        cost_estimate=pl.CostEstimate(
            flops=6 * tokens * depth * width, bytes_accessed=8 * tokens * depth, transcendentals=0
        ),
    )(features, cotangent, weight.reshape(2, half, width))


def solution(mesh):
    in_specs = (
        P(("outer", "inner"), None),
        P(("outer", "inner"), None),
        P("inner", None, None),
        P("inner", None, None),
    )
    out_specs = (
        P(("outer", "inner"), None),
        P(("outer", "inner"), None),
        P(("inner", "outer"), None),
    )
    small = mesh.shape["outer"] == 8 and mesh.shape["inner"] == 4
    return jax.shard_map(
        fused if small else on_device,
        mesh=mesh, in_specs=in_specs, out_specs=out_specs, check_vma=False,
    )
```

```python
import functools

import jax
import jax.numpy as jnp
from jax import lax
from jax.experimental import pallas as pl
from jax.experimental.pallas import tpu as pltpu
from jax.sharding import PartitionSpec as P


def dequantize(codes, scales):
    width = codes.shape[2]
    return (codes.astype(jnp.float32) * scales).astype(jnp.bfloat16).reshape(-1, width)


def forward_part(features, cotangent, w_codes, w_scales):
    weight = lax.all_gather(dequantize(w_codes, w_scales), "inner", axis=0, tiled=True)
    key_proj = jnp.dot(features, weight, preferred_element_type=jnp.float32).astype(jnp.bfloat16)
    grad_input = lax.dot_general(
        cotangent, weight, (((1,), (1,)), ((), ())), preferred_element_type=jnp.float32
    ).astype(jnp.bfloat16)
    return (key_proj, grad_input)


def gradient_part(features, cotangent, rows_block):
    width = cotangent.shape[1]
    grad_share = lax.psum_scatter(
        lax.dot_general(
            features, cotangent, (((0,), (0,)), ((), ())), preferred_element_type=jnp.float32
        ).astype(jnp.bfloat16),
        "inner",
        scatter_dimension=0,
        tiled=True,
    ).astype(jnp.float32)
    blocks = grad_share.reshape(-1, rows_block * width)
    block_scale = jnp.max(jnp.abs(blocks), axis=1, keepdims=True) + 1e-06
    block_codes = (blocks / block_scale).astype(jnp.bfloat16).reshape(-1, rows_block, width)
    got_codes, got_scales = (
        lax.all_to_all(block_codes, "outer", split_axis=0, concat_axis=0, tiled=True),
        lax.all_to_all(
            block_scale.reshape(-1, 1, 1).astype(jnp.bfloat16),
            "outer",
            split_axis=0,
            concat_axis=0,
            tiled=True,
        ).astype(jnp.float32),
    )
    senders = lax.axis_size("outer")
    devices = senders * lax.axis_size("inner")
    restored = (got_codes.astype(jnp.float32) * got_scales).reshape(senders, -1, rows_block, width)
    summed = jnp.sum(restored, axis=0).reshape(-1, width)
    return (summed / devices).astype(jnp.bfloat16)


def on_device(features, cotangent, w_codes, w_scales):
    rows_block = w_codes.shape[1]
    key_proj, grad_input = forward_part(features, cotangent, w_codes, w_scales)
    grad_weight = gradient_part(features, cotangent, rows_block)
    return (key_proj, grad_input, grad_weight)


WEIGHT_OF = {"y": 16, "core": 8, "zh": 4, "zl": 2, "x": 1}
STREAMS = (
    ("core", "x", "y", "zl", "zh"),
    ("core", "zl", "y", "x", "zh"),
    ("core", "x", "zl", "y", "zh"),
    ("core", "zl", "x", "y", "zh"),
)
CHUNKS = 4
SPLIT = 3
MESH = pl.DeviceIdType.MESH


def kernel(feat, cot, own, key_ref, gin_ref, gw_ref, part, got, held, acc, w_send, w_recv, g_send, g_recv):
    outer, inner = lax.axis_index("outer"), lax.axis_index("inner")
    bit = {
        "x": outer % 2,
        "zl": (outer // 2) % 2,
        "zh": outer // 4,
        "core": inner % 2,
        "y": inner // 2,
    }

    def flip(v, b, step):
        return v + step - 2 * step * b

    partner = {
        "x": (flip(outer, bit["x"], 1), inner),
        "zl": (flip(outer, bit["zl"], 2), inner),
        "zh": (flip(outer, bit["zh"], 4), inner),
        "core": (outer, flip(inner, bit["core"], 1)),
        "y": (outer, flip(inner, bit["y"], 2)),
    }
    barrier = pltpu.get_barrier_semaphore()
    for p in partner.values():
        pl.semaphore_signal(barrier, inc=1, device_id=p, device_id_type=MESH)
    pl.semaphore_wait(barrier, len(partner))

    rows = part.shape[2]
    cols = part.shape[3]
    half = own.shape[1]
    mine = bit["x"] + bit["zl"] - 2 * bit["x"] * bit["zl"]
    other = 1 - mine

    def remote(src, dst, send, recv, dim):
        return pltpu.make_async_remote_copy(
            src_ref=src, dst_ref=dst, send_sem=send, recv_sem=recv,
            device_id=partner[dim], device_id_type=MESH,
        )

    def w_copy(n, src, dst, dim):
        return remote(src, dst, w_send.at[n], w_recv.at[n], dim)

    def g_copy(s, sem, step, at, n):
        return remote(
            part.at[s, pl.ds(at, n)], got.at[s, pl.ds(at, n)],
            g_send.at[s, sem], g_recv.at[s, sem], STREAMS[s][step],
        )

    def chunk(ref, h, c):
        return ref.at[h, pl.ds(c * (half // CHUNKS), half // CHUNKS)]

    chunks = range(CHUNKS)
    over_core = w_copy(4 * CHUNKS, own, held.at[0], "core")
    over_y = [w_copy(c, chunk(own, mine, c), chunk(held.at[1], mine, c), "y") for c in chunks]
    onward = [
        w_copy(
            CHUNKS + c, chunk(held.at[1], mine, c), chunk(held.at[1], mine, c), ("x", "zl")[c % 2]
        )
        for c in chunks
    ]
    core_mine, core_other = [
        [
            w_copy((2 + k) * CHUNKS + c, chunk(held.at[1], h, c), chunk(held.at[2], h, c), "core")
            for c in chunks
        ]
        for k, h in enumerate((mine, other))
    ]
    streams = range(len(STREAMS))
    first = [
        [g_copy(s, 5 + step, step, 24 >> step, 8 >> step) for step in range(SPLIT)]
        for s in streams
    ]
    g = [
        [
            g_copy(s, step, step, 16 >> step, (8 if step < SPLIT else 16) >> step)
            for step in range(5)
        ]
        for s in streams
    ]

    for c in chunks:
        over_y[c].start()

    def forward(c):
        over_y[c].wait_recv()
        onward[c].start()
        core_mine[c].start()

    def across(c):
        onward[c].wait_recv()
        core_other[c].start()

    def partial(n):
        rel, rest = {}, n
        for dim in reversed(STREAMS[0]):
            rel[dim] = rest % 2
            rest = rest // 2
        block = 0
        for dim, w in WEIGHT_OF.items():
            block = block + w * (rel[dim] + bit[dim] - 2 * rel[dim] * bit[dim])
        at = pl.multiple_of(block * rows, rows)
        value = lax.dot_general(
            feat[:, pl.ds(at, rows)], cot[...], (((0,), (0,)), ((), ())),
            preferred_element_type=jnp.float32,
        ).astype(jnp.bfloat16)
        for s, order in enumerate(STREAMS):
            place = 0
            for dim in order:
                place = place * 2 + rel[dim]
            part[s, place] = value[:, s * cols:(s + 1) * cols]

    for n in range(24, 32):
        partial(n)
    first[0][0].start()
    first[2][0].start()
    for n in (18, 19, 22, 23):
        partial(n)
    first[1][0].start()
    first[3][0].start()
    for n in (16, 17, 20, 21):
        partial(n)
    for s in streams:
        g[s][0].start()
    over_core.start()
    for n in range(16):
        partial(n)

    def add(s, lo, n, base):
        @pl.loop(lo, lo + n)
        def _(j):
            part[s, j] = (
                part[s, j].astype(jnp.float32) + got[s, base + j].astype(jnp.float32)
            ).astype(jnp.bfloat16)

    def advance_all(step):
        n = 16 >> step
        for s in streams:
            (first[s] if step < SPLIT else g[s])[step].wait_recv()
            add(s, n // 2, n // 2, n)
            if step + 1 < SPLIT:
                first[s][step + 1].start()
            g[s][step + 1].start()
        for s in streams:
            if step < SPLIT:
                g[s][step].wait_recv()
            add(s, 0, n // 2, n)

    def finish(s):
        g[s][4].wait_recv()
        total = part[s, 0].astype(jnp.float32) + got[s, 1].astype(jnp.float32)
        devices = lax.axis_size("outer") * lax.axis_size("inner")
        gw_ref[:, s * cols:(s + 1) * cols] = (total / devices).astype(jnp.bfloat16)

    flipped_core = flip(inner, bit["core"], 1)
    flipped_y = flip(inner, bit["y"], 2)
    flipped_both = flip(flipped_core, bit["y"], 2)

    def unit(block, shard, h, first=False):
        at = pl.multiple_of((shard * 2 + h) * half, half)
        value = jnp.dot(feat[:, pl.ds(at, half)], block[...], preferred_element_type=jnp.float32)
        acc[...] = value if first else acc[...] + value
        gin_ref[:, pl.ds(at, half)] = lax.dot_general(
            cot[...], block[...], (((1,), (1,)), ((), ())), preferred_element_type=jnp.float32
        ).astype(jnp.bfloat16)

    forward(0)
    advance_all(0)
    forward(1)
    unit(own.at[0], inner, 0, first=True)
    unit(own.at[1], inner, 1)
    over_core.wait_recv()
    unit(held.at[0, 0], flipped_core, 0)
    unit(held.at[0, 1], flipped_core, 1)
    for c in range(2, CHUNKS):
        forward(c)
    unit(held.at[1, mine], flipped_y, mine)
    advance_all(1)
    for c in chunks:
        core_mine[c].wait_recv()
    unit(held.at[2, mine], flipped_both, mine)
    across(0)
    across(1)
    advance_all(2)
    for c in range(2, CHUNKS):
        across(c)
    advance_all(3)
    unit(held.at[1, other], flipped_y, other)
    for c in chunks:
        core_other[c].wait_recv()
    unit(held.at[2, other], flipped_both, other)
    key_ref[...] = acc[...].astype(jnp.bfloat16)
    for s in streams:
        finish(s)
    for copy in (over_core, *over_y, *onward, *core_mine, *core_other, *sum(first, []), *sum(g, [])):
        copy.wait_send()


def fused(features, cotangent, w_codes, w_scales):
    tokens, depth = features.shape
    width = cotangent.shape[1]
    weight = dequantize(w_codes, w_scales)
    half = weight.shape[0] // 2
    rows = depth // 32
    cols = width // len(STREAMS)
    bf16 = jnp.bfloat16
    vmem = pl.BlockSpec(memory_space=pltpu.VMEM)
    return pl.pallas_call(
        kernel,
        out_shape=(
            jax.ShapeDtypeStruct((tokens, width), bf16),
            jax.ShapeDtypeStruct((tokens, depth), bf16),
            jax.ShapeDtypeStruct((rows, width), bf16),
        ),
        in_specs=[vmem] * 3,
        out_specs=(vmem,) * 3,
        scratch_shapes=[
            pltpu.VMEM((len(STREAMS), 32, rows, cols), bf16),
            pltpu.VMEM((len(STREAMS), 32, rows, cols), bf16),
            pltpu.VMEM((3, 2, half, width), bf16),
            pltpu.VMEM((tokens, width), jnp.float32),
            pltpu.SemaphoreType.DMA((4 * CHUNKS + 1,)),
            pltpu.SemaphoreType.DMA((4 * CHUNKS + 1,)),
            pltpu.SemaphoreType.DMA((len(STREAMS), 5 + SPLIT)),
            pltpu.SemaphoreType.DMA((len(STREAMS), 5 + SPLIT)),
        ],
        compiler_params=pltpu.CompilerParams(
            collective_id=0, has_side_effects=True, vmem_limit_bytes=40 * 1024 * 1024
        ),
        cost_estimate=pl.CostEstimate(
            flops=6 * tokens * depth * width, bytes_accessed=8 * tokens * depth, transcendentals=0
        ),
    )(features, cotangent, weight.reshape(2, half, width))


def solution(mesh):
    in_specs = (
        P(("outer", "inner"), None),
        P(("outer", "inner"), None),
        P("inner", None, None),
        P("inner", None, None),
    )
    out_specs = (
        P(("outer", "inner"), None),
        P(("outer", "inner"), None),
        P(("inner", "outer"), None),
    )
    small = mesh.shape["outer"] == 8 and mesh.shape["inner"] == 4
    return jax.shard_map(
        fused if small else on_device,
        mesh=mesh, in_specs=in_specs, out_specs=out_specs, check_vma=False,
    )
```

```python
import functools

import jax
import jax.numpy as jnp
from jax import lax
from jax.experimental import pallas as pl
from jax.experimental.pallas import tpu as pltpu
from jax.sharding import PartitionSpec as P


def dequantize(codes, scales):
    width = codes.shape[2]
    return (codes.astype(jnp.float32) * scales).astype(jnp.bfloat16).reshape(-1, width)


def forward_part(features, cotangent, w_codes, w_scales):
    weight = lax.all_gather(dequantize(w_codes, w_scales), "inner", axis=0, tiled=True)
    key_proj = jnp.dot(features, weight, preferred_element_type=jnp.float32).astype(jnp.bfloat16)
    grad_input = lax.dot_general(
        cotangent, weight, (((1,), (1,)), ((), ())), preferred_element_type=jnp.float32
    ).astype(jnp.bfloat16)
    return (key_proj, grad_input)


def gradient_part(features, cotangent, rows_block):
    width = cotangent.shape[1]
    grad_share = lax.psum_scatter(
        lax.dot_general(
            features, cotangent, (((0,), (0,)), ((), ())), preferred_element_type=jnp.float32
        ).astype(jnp.bfloat16),
        "inner",
        scatter_dimension=0,
        tiled=True,
    ).astype(jnp.float32)
    blocks = grad_share.reshape(-1, rows_block * width)
    block_scale = jnp.max(jnp.abs(blocks), axis=1, keepdims=True) + 1e-06
    block_codes = (blocks / block_scale).astype(jnp.bfloat16).reshape(-1, rows_block, width)
    got_codes, got_scales = (
        lax.all_to_all(block_codes, "outer", split_axis=0, concat_axis=0, tiled=True),
        lax.all_to_all(
            block_scale.reshape(-1, 1, 1).astype(jnp.bfloat16),
            "outer",
            split_axis=0,
            concat_axis=0,
            tiled=True,
        ).astype(jnp.float32),
    )
    senders = lax.axis_size("outer")
    devices = senders * lax.axis_size("inner")
    restored = (got_codes.astype(jnp.float32) * got_scales).reshape(senders, -1, rows_block, width)
    summed = jnp.sum(restored, axis=0).reshape(-1, width)
    return (summed / devices).astype(jnp.bfloat16)


def on_device(features, cotangent, w_codes, w_scales):
    rows_block = w_codes.shape[1]
    key_proj, grad_input = forward_part(features, cotangent, w_codes, w_scales)
    grad_weight = gradient_part(features, cotangent, rows_block)
    return (key_proj, grad_input, grad_weight)


WEIGHT_OF = {"y": 16, "core": 8, "zh": 4, "zl": 2, "x": 1}
STREAMS = (
    ("core", "x", "y", "zl", "zh"),
    ("core", "zl", "y", "x", "zh"),
    ("core", "x", "zl", "y", "zh"),
    ("core", "y", "zl", "x", "zh"),
)
CHUNKS = 4
SPLIT = 3
MESH = pl.DeviceIdType.MESH


def kernel(feat, cot, own, key_ref, gin_ref, gw_ref, part, got, held, acc, w_send, w_recv, g_send, g_recv):
    outer, inner = lax.axis_index("outer"), lax.axis_index("inner")
    bit = {
        "x": outer % 2,
        "zl": (outer // 2) % 2,
        "zh": outer // 4,
        "core": inner % 2,
        "y": inner // 2,
    }

    def flip(v, b, step):
        return v + step - 2 * step * b

    partner = {
        "x": (flip(outer, bit["x"], 1), inner),
        "zl": (flip(outer, bit["zl"], 2), inner),
        "zh": (flip(outer, bit["zh"], 4), inner),
        "core": (outer, flip(inner, bit["core"], 1)),
        "y": (outer, flip(inner, bit["y"], 2)),
    }
    barrier = pltpu.get_barrier_semaphore()
    for p in partner.values():
        pl.semaphore_signal(barrier, inc=1, device_id=p, device_id_type=MESH)
    pl.semaphore_wait(barrier, len(partner))

    rows = part.shape[2]
    cols = part.shape[3]
    half = own.shape[1]
    mine = bit["x"] + bit["zl"] - 2 * bit["x"] * bit["zl"]
    other = 1 - mine

    def remote(src, dst, send, recv, dim):
        return pltpu.make_async_remote_copy(
            src_ref=src, dst_ref=dst, send_sem=send, recv_sem=recv,
            device_id=partner[dim], device_id_type=MESH,
        )

    def w_copy(n, src, dst, dim):
        return remote(src, dst, w_send.at[n], w_recv.at[n], dim)

    def g_copy(s, sem, step, at, n):
        return remote(
            part.at[s, pl.ds(at, n)], got.at[s, pl.ds(at, n)],
            g_send.at[s, sem], g_recv.at[s, sem], STREAMS[s][step],
        )

    def chunk(ref, h, c):
        return ref.at[h, pl.ds(c * (half // CHUNKS), half // CHUNKS)]

    chunks = range(CHUNKS)
    over_core = w_copy(4 * CHUNKS, own, held.at[0], "core")
    over_y = [w_copy(c, chunk(own, mine, c), chunk(held.at[1], mine, c), "y") for c in chunks]
    onward = [
        w_copy(
            CHUNKS + c, chunk(held.at[1], mine, c), chunk(held.at[1], mine, c), ("x", "zl")[c % 2]
        )
        for c in chunks
    ]
    core_mine, core_other = [
        [
            w_copy((2 + k) * CHUNKS + c, chunk(held.at[1], h, c), chunk(held.at[2], h, c), "core")
            for c in chunks
        ]
        for k, h in enumerate((mine, other))
    ]
    streams = range(len(STREAMS))
    first = [
        [g_copy(s, 5 + step, step, 24 >> step, 8 >> step) for step in range(SPLIT)]
        for s in streams
    ]
    g = [
        [
            g_copy(s, step, step, 16 >> step, (8 if step < SPLIT else 16) >> step)
            for step in range(5)
        ]
        for s in streams
    ]

    for c in chunks:
        over_y[c].start()

    def forward(c):
        over_y[c].wait_recv()
        onward[c].start()
        core_mine[c].start()

    def across(c):
        onward[c].wait_recv()
        core_other[c].start()

    def partial(n):
        rel, rest = {}, n
        for dim in reversed(STREAMS[0]):
            rel[dim] = rest % 2
            rest = rest // 2
        block = 0
        for dim, w in WEIGHT_OF.items():
            block = block + w * (rel[dim] + bit[dim] - 2 * rel[dim] * bit[dim])
        at = pl.multiple_of(block * rows, rows)
        value = lax.dot_general(
            feat[:, pl.ds(at, rows)], cot[...], (((0,), (0,)), ((), ())),
            preferred_element_type=jnp.float32,
        ).astype(jnp.bfloat16)
        for s, order in enumerate(STREAMS):
            place = 0
            for dim in order:
                place = place * 2 + rel[dim]
            part[s, place] = value[:, s * cols:(s + 1) * cols]

    for n in range(24, 32):
        partial(n)
    first[0][0].start()
    first[2][0].start()
    for n in range(20, 24):
        partial(n)
    first[3][0].start()
    for n in (18, 19):
        partial(n)
    first[1][0].start()
    for n in (16, 17):
        partial(n)
    for s in streams:
        g[s][0].start()
    over_core.start()
    for n in range(16):
        partial(n)

    def add(s, lo, n, base):
        @pl.loop(lo, lo + n)
        def _(j):
            part[s, j] = (
                part[s, j].astype(jnp.float32) + got[s, base + j].astype(jnp.float32)
            ).astype(jnp.bfloat16)

    def advance_all(step):
        n = 16 >> step
        for s in streams:
            (first[s] if step < SPLIT else g[s])[step].wait_recv()
            add(s, n // 2, n // 2, n)
            if step + 1 < SPLIT:
                first[s][step + 1].start()
            g[s][step + 1].start()
        for s in streams:
            if step < SPLIT:
                g[s][step].wait_recv()
            add(s, 0, n // 2, n)

    def finish(s):
        g[s][4].wait_recv()
        total = part[s, 0].astype(jnp.float32) + got[s, 1].astype(jnp.float32)
        devices = lax.axis_size("outer") * lax.axis_size("inner")
        gw_ref[:, s * cols:(s + 1) * cols] = (total / devices).astype(jnp.bfloat16)

    flipped_core = flip(inner, bit["core"], 1)
    flipped_y = flip(inner, bit["y"], 2)
    flipped_both = flip(flipped_core, bit["y"], 2)

    def unit(block, shard, h, first=False):
        at = pl.multiple_of((shard * 2 + h) * half, half)
        value = jnp.dot(feat[:, pl.ds(at, half)], block[...], preferred_element_type=jnp.float32)
        acc[...] = value if first else acc[...] + value
        gin_ref[:, pl.ds(at, half)] = lax.dot_general(
            cot[...], block[...], (((1,), (1,)), ((), ())), preferred_element_type=jnp.float32
        ).astype(jnp.bfloat16)

    forward(0)
    advance_all(0)
    forward(1)
    unit(own.at[0], inner, 0, first=True)
    unit(own.at[1], inner, 1)
    over_core.wait_recv()
    unit(held.at[0, 0], flipped_core, 0)
    unit(held.at[0, 1], flipped_core, 1)
    for c in range(2, CHUNKS):
        forward(c)
    unit(held.at[1, mine], flipped_y, mine)
    advance_all(1)
    for c in chunks:
        core_mine[c].wait_recv()
    unit(held.at[2, mine], flipped_both, mine)
    across(0)
    across(1)
    advance_all(2)
    for c in range(2, CHUNKS):
        across(c)
    advance_all(3)
    unit(held.at[1, other], flipped_y, other)
    for c in chunks:
        core_other[c].wait_recv()
    unit(held.at[2, other], flipped_both, other)
    key_ref[...] = acc[...].astype(jnp.bfloat16)
    for s in streams:
        finish(s)
    for copy in (over_core, *over_y, *onward, *core_mine, *core_other, *sum(first, []), *sum(g, [])):
        copy.wait_send()


def fused(features, cotangent, w_codes, w_scales):
    tokens, depth = features.shape
    width = cotangent.shape[1]
    weight = dequantize(w_codes, w_scales)
    half = weight.shape[0] // 2
    rows = depth // 32
    cols = width // len(STREAMS)
    bf16 = jnp.bfloat16
    vmem = pl.BlockSpec(memory_space=pltpu.VMEM)
    return pl.pallas_call(
        kernel,
        out_shape=(
            jax.ShapeDtypeStruct((tokens, width), bf16),
            jax.ShapeDtypeStruct((tokens, depth), bf16),
            jax.ShapeDtypeStruct((rows, width), bf16),
        ),
        in_specs=[vmem] * 3,
        out_specs=(vmem,) * 3,
        scratch_shapes=[
            pltpu.VMEM((len(STREAMS), 32, rows, cols), bf16),
            pltpu.VMEM((len(STREAMS), 32, rows, cols), bf16),
            pltpu.VMEM((3, 2, half, width), bf16),
            pltpu.VMEM((tokens, width), jnp.float32),
            pltpu.SemaphoreType.DMA((4 * CHUNKS + 1,)),
            pltpu.SemaphoreType.DMA((4 * CHUNKS + 1,)),
            pltpu.SemaphoreType.DMA((len(STREAMS), 5 + SPLIT)),
            pltpu.SemaphoreType.DMA((len(STREAMS), 5 + SPLIT)),
        ],
        compiler_params=pltpu.CompilerParams(
            collective_id=0, has_side_effects=True, vmem_limit_bytes=40 * 1024 * 1024
        ),
        cost_estimate=pl.CostEstimate(
            flops=6 * tokens * depth * width, bytes_accessed=8 * tokens * depth, transcendentals=0
        ),
    )(features, cotangent, weight.reshape(2, half, width))


def solution(mesh):
    in_specs = (
        P(("outer", "inner"), None),
        P(("outer", "inner"), None),
        P("inner", None, None),
        P("inner", None, None),
    )
    out_specs = (
        P(("outer", "inner"), None),
        P(("outer", "inner"), None),
        P(("inner", "outer"), None),
    )
    small = mesh.shape["outer"] == 8 and mesh.shape["inner"] == 4
    return jax.shard_map(
        fused if small else on_device,
        mesh=mesh, in_specs=in_specs, out_specs=out_specs, check_vma=False,
    )
```
